128 devices in a mesh: aux: 16 (over z_lo, x, core), orb: 8 (over y, z_hi).
Axes of the slice: x: 4, y: 4, z: 4 (z_hi: 2, z_lo: 2; z = z_hi * 2 + z_lo), core: 2. Of those that a mesh axis runs over, the one named last changes fastest.
Arguments:
- b_factors: float32 [16, 1024, 20480], P('aux', None, 'orb'), may hold values from -6 to 6
- occupied: float32 [20480, 2048], P('orb', 'aux'), may hold values from -0.0390625 to 0.0390625
- b_mask: int32 [16, 8, 160], P('aux', None, 'orb'), may hold values 0 or 1
- c_mask: int32 [160, 16], P('orb', 'aux'), may hold values 0 or 1
Outputs:
- exchange: float32 [1024, 1024], P('orb')
The draws below stay inside these ranges and needn't reach their ends.
All inputs are finite; a program needn't handle non-finite values. No bound on the sum of `b_mask` or of `c_mask` on one device may be relied on, other than what follows from the above.
Results may differ from the reference program's by a relative error of at most 0.0001.
Values sent between devices are 32-bit elements; how exact they have to be, the bound alone decides.
No kernel may reach another device: no remote copies, remote signals or barrier semaphores. Data moves between devices by JAX's collectives and lax.ppermute only.
A program may use at most 128 MiB of HBM per device.

```python
import math
import jax
import jax.numpy as jnp
from jax import lax

BLK = 128
LAM = 20480
NOCC = 2048
M = 1024
NAUX = 16


def set_ends(result, own_key, low, largest):
    longest = result.shape.index(max(result.shape))
    spots = []
    for shift in (0, 1):
        where = [jax.random.randint(jax.random.fold_in(own_key, axis), (), 0, length) for axis, length in enumerate(result.shape)]
        where[longest] = (where[longest] + shift) % result.shape[longest]
        spots.append(tuple(where))
    return result.at[spots[0]].set(low).at[spots[1]].set(largest)


def block_levels(own_key, dims, cuts, smallest, high):
    level, own = 1.0, jax.random.fold_in(own_key, 6)
    for dim, blocks in cuts:
        draws = jnp.exp(jax.random.uniform(jax.random.fold_in(own, dim), (blocks,), jnp.float32, smallest / len(cuts), high / len(cuts)))
        level = level * jnp.repeat(draws, dims[dim] // blocks).reshape([-1 if axis == dim else 1 for axis in range(len(dims))])
    return level


def bell_draw(own_key, dims, scale, reach, shards=(), kind=jnp.bfloat16):
    level = block_levels(own_key, dims, shards, -0.22, 0.18) if shards else 1.0
    drawn = jax.random.normal(own_key, dims, jnp.float32) * scale * level
    return jnp.minimum(jnp.maximum(drawn, -reach), reach).astype(kind)


def setup_inputs(seed: int = 0) -> dict:
    keys = jax.random.split(jax.random.key(seed), 5)
    return {
        "b_factors": bell_draw(keys[0], (NAUX, M, LAM), 1.0, 6.0, ((0, 16), (2, 8)), jnp.float32),
        "occupied": bell_draw(keys[1], (LAM, NOCC), LAM ** -0.5, 0.0390625, ((0, 8), (1, 16)), jnp.float32),
        "b_mask": set_ends((jax.random.randint(keys[2], (NAUX, M // BLK, LAM // BLK), 0, 4) < 3).astype(jnp.int32), jax.random.fold_in(keys[2], 1), 0, 1),
        "c_mask": set_ends((jax.random.randint(keys[3], (LAM // BLK, NOCC // BLK), 0, 3) < 2).astype(jnp.int32), jax.random.fold_in(keys[3], 1), 0, 1),
    }


def expand(mask_blocks):
    spread = jnp.repeat(mask_blocks.astype(jnp.float32), BLK, axis=-2)
    return jnp.repeat(spread, BLK, axis=-1)

def reference(b_factors, occupied, b_mask, c_mask):
    masked_occ = occupied * expand(c_mask)

    def accumulate(summed, inputs):
        factors_q, mask_q = inputs
        fitted = jnp.dot(factors_q * expand(mask_q), masked_occ, precision=lax.Precision.HIGHEST, preferred_element_type=jnp.float32)
        return (summed + jnp.dot(fitted, fitted.T, precision=lax.Precision.HIGHEST, preferred_element_type=jnp.float32), None)
    start = jnp.zeros((M, M), jnp.float32)
    summed, unused = lax.scan(accumulate, start, (b_factors, b_mask))
    return summed * (1.0 / math.sqrt(NAUX * NOCC))
```

```python
import functools
import math

import jax
import jax.numpy as jnp
from jax import lax
from jax.experimental import pallas as pl
from jax.experimental.pallas import tpu as pltpu
from jax.sharding import PartitionSpec as P

BLK = 128
NOCC = 2048
F32 = jnp.float32
BF16 = jnp.bfloat16
VMEM_LIMIT = 56 * 1024 * 1024
NT = (((1,), (1,)), ((), ()))


def aux_pairs(move):
    pairs = []
    for z in range(2):
        for x in range(4):
            for core in range(2):
                z2, x2, core2 = move(z, x, core)
                pairs.append((z * 8 + x * 2 + core, z2 * 8 + (x2 % 4) * 2 + core2))
    return pairs


def orb_pairs(move):
    pairs = []
    for y in range(4):
        for h in range(2):
            y2, h2 = move(y, h)
            pairs.append((y * 2 + h, (y2 % 4) * 2 + h2))
    return pairs


MOVES = {
    "x+": ("aux", aux_pairs(lambda z, x, c: (z, x + 1, c))),
    "x-": ("aux", aux_pairs(lambda z, x, c: (z, x - 1, c))),
    "xa": ("aux", aux_pairs(lambda z, x, c: (z, x ^ 1, c))),
    "xb": ("aux", aux_pairs(lambda z, x, c: (z, 3 - x, c))),
    "zl": ("aux", aux_pairs(lambda z, x, c: (1 - z, x, c))),
    "core": ("aux", aux_pairs(lambda z, x, c: (z, x, 1 - c))),
    "y+": ("orb", orb_pairs(lambda y, h: (y + 1, h))),
    "y-": ("orb", orb_pairs(lambda y, h: (y - 1, h))),
    "zh": ("orb", orb_pairs(lambda y, h: (y, 1 - h))),
}


def move(value, name):
    axis, pairs = MOVES[name]
    return lax.ppermute(value, axis, pairs)


def params():
    return pltpu.CompilerParams(vmem_limit_bytes=VMEM_LIMIT)


def whole(shape):
    return pl.BlockSpec(shape, lambda *_: tuple(0 for _ in shape))


SMEM = pl.BlockSpec(memory_space=pltpu.SMEM)

SEGMENTS = ((2, 0), (1, 1), (2, 1), (3, 0), (1, 0), (3, 1), (0, 0), (0, 1))
GROUPS = (2, 2, 1, 1, 2)


def transpose_panel(occupied, c_mask):
    depth, width = occupied.shape

    def kernel(mask_ref, c_ref, out_ref):
        for k in range(depth // BLK):
            keep = mask_ref[k, 0].astype(F32)
            out_ref[:, k * BLK : (k + 1) * BLK] = (c_ref[k * BLK : (k + 1) * BLK, :] * keep).T

    return pl.pallas_call(
        kernel,
        out_shape=jax.ShapeDtypeStruct((width, depth), F32),
        in_specs=[SMEM, whole(occupied.shape)],
        out_specs=whole((width, depth)),
        compiler_params=params(),
        name="panel",
    )(c_mask, occupied)


def split_factors(factors, mask):
    rows, depth = factors.shape

    def kernel(mask_ref, b_ref, hi_ref, lo_ref):
        row = pl.program_id(0)
        for k in range(depth // BLK):
            cols = slice(k * BLK, (k + 1) * BLK)
            value = b_ref[:, cols] * mask_ref[row, k]
            hi = value.astype(BF16)
            hi_ref[:, cols] = hi
            lo_ref[:, cols] = (value - hi.astype(F32)).astype(BF16)

    block = pl.BlockSpec((BLK, depth), lambda i: (i, 0))
    return pl.pallas_call(
        kernel,
        grid=(rows // BLK,),
        out_shape=[jax.ShapeDtypeStruct((rows, depth), BF16)] * 2,
        in_specs=[SMEM, block],
        out_specs=[block, block],
        compiler_params=params(),
        name="split",
    )(mask, factors)


def fitted_chunk(place, pieces, factors):
    own_hi, own_lo, other_hi, other_lo = factors
    rows, depth = own_hi.shape
    total = sum(piece.shape[0] for piece in pieces)
    seg = total // 8
    tile = 256
    steps = rows // tile
    count = len(pieces)

    def kernel(place_ref, *refs):
        piece_refs = refs[:count]
        own_hi_ref, own_lo_ref, other_hi_ref, other_lo_ref = refs[count : count + 4]
        out_refs = refs[count + 4 : count + 9]
        panel = refs[count + 9]
        step = pl.program_id(0)

        @pl.when(step == 0)
        def _():
            y, h = place_ref[0], place_ref[1]
            for index, (ahead, half) in enumerate(SEGMENTS):
                shard = lax.rem(y + ahead, 4)
                side = h if half == 0 else 1 - h
                parts = []
                for ref in piece_refs:
                    length = ref.shape[0] // 8
                    first = pl.multiple_of((shard * 2 + side) * length, length)
                    parts.append(ref[pl.ds(first, length), :])
                value = parts[0] if count == 1 else jnp.concatenate(parts, axis=0)
                hi = value.astype(BF16)
                panel[index * seg : (index + 1) * seg, :] = hi
                panel[total + index * seg : total + (index + 1) * seg, :] = (
                    value - hi.astype(F32)
                ).astype(BF16)

        def product(hi_ref, lo_ref):
            both = lax.dot_general(panel[...], hi_ref[...], NT, preferred_element_type=F32)
            rest = lax.dot_general(panel[:total, :], lo_ref[...], NT, preferred_element_type=F32)
            value = both[:total] + (both[total:] + rest)
            first = 0
            for ref, size in zip(out_refs, GROUPS):
                ref[...] = value[first * seg : (first + size) * seg, :]
                first += size

        @pl.when(step < steps)
        def _():
            product(own_hi_ref, own_lo_ref)

        @pl.when(step >= steps)
        def _():
            product(other_hi_ref, other_lo_ref)

    own_spec = pl.BlockSpec((tile, depth), lambda i: (jnp.minimum(i, steps - 1), 0))
    other_spec = pl.BlockSpec((tile, depth), lambda i: (jnp.maximum(i - steps, 0), 0))
    return pl.pallas_call(
        kernel,
        grid=(2 * steps,),
        out_shape=[jax.ShapeDtypeStruct((size * seg, 2 * rows), F32) for size in GROUPS],
        in_specs=[SMEM]
        + [whole(piece.shape) for piece in pieces]
        + [own_spec, own_spec, other_spec, other_spec],
        out_specs=[pl.BlockSpec((size * seg, tile), lambda i: (0, i)) for size in GROUPS],
        scratch_shapes=[pltpu.VMEM((2 * total, depth), BF16)],
        compiler_params=params(),
        cost_estimate=pl.CostEstimate(
            flops=6 * total * 2 * rows * depth, bytes_accessed=8 * rows * depth, transcendentals=0
        ),
        name="fitted",
    )(place, *pieces, own_hi, own_lo, other_hi, other_lo)


def exchange_partial(place, kept, arrived, scale):
    rows = sum(part.shape[0] for part in kept)
    width = kept[0].shape[1] // 2
    half_width = width // 2
    count = len(kept)

    def kernel(place_ref, *refs):
        kept_refs, arrived_refs = refs[:count], refs[count : 2 * count]
        send_ref = refs[2 * count]
        out_refs = refs[2 * count + 1 : 2 * count + 6]
        full, hi_ref, lo_ref = refs[2 * count + 6 :]
        y, h, core = place_ref[0], place_ref[1], place_ref[2]
        first = 0
        for kept_ref, arrived_ref in zip(kept_refs, arrived_refs):
            length = kept_ref.shape[0]
            value = kept_ref[...] + arrived_ref[...]
            full[first : first + length, :] = value[:, :width]
            full[rows + first : rows + first + length, :] = value[:, width:]
            first += length
        value = full[...]
        hi = value.astype(BF16)
        hi_ref[...] = hi
        lo_ref[...] = (value - hi.astype(F32)).astype(BF16)
        mine = pl.ds(pl.multiple_of(core * half_width, half_width), half_width)
        theirs = pl.ds(pl.multiple_of((1 - core) * half_width, half_width), half_width)

        def product(left, columns):
            left_hi = left.astype(BF16)
            left_lo = (left - left_hi.astype(F32)).astype(BF16)
            right_hi, right_lo = hi_ref[:, columns], lo_ref[:, columns]
            value = jnp.dot(left_hi, right_hi, preferred_element_type=F32)
            value += jnp.dot(left_hi, right_lo, preferred_element_type=F32)
            value += jnp.dot(left_lo, right_hi, preferred_element_type=F32)
            return value * scale

        index = 0
        for ref, size in zip(out_refs, GROUPS):
            for part in range(size):
                ahead, half = SEGMENTS[index]
                side = h if half == 0 else 1 - h
                block = lax.rem(y + ahead, 4) * 2 + side
                left = full[:, pl.ds(pl.multiple_of(block * BLK, BLK), BLK)].T
                ref[part * BLK : (part + 1) * BLK, :] = product(left, mine)
                send_ref[index * BLK : (index + 1) * BLK, :] = product(left, theirs)
                index += 1

    shapes = [(width, half_width)] + [(size * BLK, half_width) for size in GROUPS]
    return pl.pallas_call(
        kernel,
        out_shape=[jax.ShapeDtypeStruct(shape, F32) for shape in shapes],
        in_specs=[SMEM] + [whole(part.shape) for part in (*kept, *arrived)],
        out_specs=[whole(shape) for shape in shapes],
        scratch_shapes=[
            pltpu.VMEM((2 * rows, width), F32),
            pltpu.VMEM((2 * rows, width), BF16),
            pltpu.VMEM((2 * rows, width), BF16),
        ],
        compiler_params=params(),
        name="exchange",
    )(place, *kept, *arrived)


def scatter_y(parts):
    plus, minus, plus_late, minus_late, own = parts
    seg = plus_late.shape[0]
    from_below, from_above = move(plus, "y+"), move(minus, "y-")
    late_below = move(plus_late + from_below[:seg], "y+")
    late_above = move(minus_late + from_above[:seg], "y-")
    sent = own[seg:] + from_below[seg:] + late_above
    kept = own[:seg] + from_above[seg:] + late_below
    return kept, sent


def body(b_factors, occupied, b_mask, c_mask):
    aux, orb = lax.axis_index("aux"), lax.axis_index("orb")
    core = lax.rem(aux, 2)
    place = jnp.stack([lax.div(orb, 2), lax.rem(orb, 2), core]).astype(jnp.int32)
    naux = lax.axis_size("aux")
    factor = 1.0 / math.sqrt(b_factors.shape[0] * naux * NOCC)
    own_b, own_mask = b_factors[0], b_mask[0].astype(F32)

    panel = transpose_panel(occupied, c_mask)
    left, right, across = move(panel, "x+"), move(panel, "x-"), move(panel, "zl")
    other_b, other_mask = move(own_b, "core"), move(own_mask, "core")
    factors = (*split_factors(own_b, own_mask), *split_factors(other_b, other_mask))

    left2 = move(across, "x+")
    far = move(right, "x-")
    right2 = move(right, "zl")
    half = panel.shape[0] // 2
    far2 = (move(left2[:half], "x+"), move(right2[half:], "x-"))

    kept, arrived = [], []
    for pieces in ((panel,), (left, right, across), (left2, far, right2), far2):
        stay, sent = scatter_y(fitted_chunk(place, pieces, factors))
        kept.append(stay)
        arrived.append(move(sent, "zh"))

    send, *parts = exchange_partial(place, kept, arrived, factor)
    other = move(send, "core")
    first, summed = 0, []
    for part in parts:
        size = part.shape[0]
        summed.append(part + other[first : first + size])
        first += size
    stay, sent = scatter_y(summed)
    block = stay + move(sent, "zh")
    for name in ("zl", "xa", "xb"):
        block = block + move(block, name)
    other = move(block, "core")
    low = jnp.where(core == 0, block, other)
    high = jnp.where(core == 0, other, block)
    return jnp.concatenate([low, high], axis=1)


def solution(mesh):
    placed = (P("aux", None, "orb"), P("orb", "aux"), P("aux", None, "orb"), P("orb", "aux"))
    return jax.shard_map(
        body, mesh=mesh, in_specs=placed, out_specs=P("orb", None), check_vma=False
    )
```

```python
import functools
import math

import jax
import jax.numpy as jnp
from jax import lax
from jax.experimental import pallas as pl
from jax.experimental.pallas import tpu as pltpu
from jax.sharding import PartitionSpec as P

BLK = 128
NOCC = 2048
F32 = jnp.float32
BF16 = jnp.bfloat16
MIB = 1024 * 1024
NT = (((1,), (1,)), ((), ()))


def aux_pairs(move):
    pairs = []
    for z in range(2):
        for x in range(4):
            for core in range(2):
                z2, x2, core2 = move(z, x, core)
                pairs.append((z * 8 + x * 2 + core, z2 * 8 + (x2 % 4) * 2 + core2))
    return pairs


def orb_pairs(move):
    pairs = []
    for y in range(4):
        for h in range(2):
            y2, h2 = move(y, h)
            pairs.append((y * 2 + h, (y2 % 4) * 2 + h2))
    return pairs


MOVES = {
    "x+": ("aux", aux_pairs(lambda z, x, c: (z, x + 1, c))),
    "x-": ("aux", aux_pairs(lambda z, x, c: (z, x - 1, c))),
    "xa": ("aux", aux_pairs(lambda z, x, c: (z, x ^ 1, c))),
    "xb": ("aux", aux_pairs(lambda z, x, c: (z, 3 - x, c))),
    "zl": ("aux", aux_pairs(lambda z, x, c: (1 - z, x, c))),
    "core": ("aux", aux_pairs(lambda z, x, c: (z, x, 1 - c))),
    "y+": ("orb", orb_pairs(lambda y, h: (y + 1, h))),
    "y-": ("orb", orb_pairs(lambda y, h: (y - 1, h))),
    "zh": ("orb", orb_pairs(lambda y, h: (y, 1 - h))),
}


def move(value, name):
    axis, pairs = MOVES[name]
    return lax.ppermute(value, axis, pairs)


def params(mib):
    return pltpu.CompilerParams(vmem_limit_bytes=mib * MIB)


def whole(shape):
    return pl.BlockSpec(shape, lambda *_: tuple(0 for _ in shape))


SMEM = pl.BlockSpec(memory_space=pltpu.SMEM)
VMEM = pl.BlockSpec(memory_space=pltpu.VMEM)
ANY = pl.BlockSpec(memory_space=pl.ANY)


def shape_of(rows, columns):
    return jax.ShapeDtypeStruct((rows, columns), F32)


def after(values, *earlier):
    count = len(values)

    def kernel(*refs):
        del refs

    return pl.pallas_call(
        kernel,
        out_shape=[jax.ShapeDtypeStruct(value.shape, value.dtype) for value in values],
        in_specs=[ANY] * (count + len(earlier)),
        out_specs=[ANY] * count,
        input_output_aliases={index: index for index in range(count)},
        compiler_params=params(1),
        name="after",
    )(*values, *earlier)

SEGMENTS = ((2, 0), (1, 1), (2, 1), (3, 0), (1, 0), (3, 1), (0, 0), (0, 1))
GROUPS = (2, 2, 1, 1, 2)


def transpose_panel(occupied, c_mask):
    depth, width = occupied.shape
    half = width // 2

    def kernel(mask_ref, c_ref, first_ref, second_ref):
        for k in range(depth // BLK):
            rows = slice(k * BLK, (k + 1) * BLK)
            block = (c_ref[rows, :] * mask_ref[k, 0].astype(F32)).T
            first_ref[:, rows] = block[:half]
            second_ref[:, rows] = block[half:]

    return pl.pallas_call(
        kernel,
        out_shape=[shape_of(half, depth)] * 2,
        in_specs=[SMEM, VMEM],
        out_specs=[VMEM] * 2,
        compiler_params=params(8),
        name="panel",
    )(c_mask, occupied)


def split_factors(factors, mask):
    rows, depth = factors.shape

    def kernel(mask_ref, b_ref, hi_ref, lo_ref):
        row = pl.program_id(0)
        here = pl.ds(pl.multiple_of(row * BLK, BLK), BLK)
        for k in range(depth // BLK):
            cols = slice(k * BLK, (k + 1) * BLK)
            value = b_ref[:, cols] * mask_ref[row, k]
            hi = value.astype(BF16)
            hi_ref[here, cols] = hi
            lo_ref[here, cols] = (value - hi.astype(F32)).astype(BF16)

    return pl.pallas_call(
        kernel,
        grid=(rows // BLK,),
        out_shape=[pltpu.VMEM((rows, depth), BF16)] * 2,
        in_specs=[SMEM, pl.BlockSpec((BLK, depth), lambda i: (i, 0))],
        out_specs=[VMEM, VMEM],
        compiler_params=params(8),
        name="split",
    )(mask, factors)


def fitted_chunk(place, pieces, factors, earlier):
    rows, depth = factors[0].shape
    total = sum(piece.shape[0] for piece in pieces)
    seg = total // 8
    tile = 256
    count = len(pieces)

    def kernel(place_ref, *refs):
        piece_refs = refs[:count]
        factor_refs = refs[count : count + 4]
        out_refs = refs[-6:-1]
        panel = refs[-1]
        y = place_ref[0]
        for index, (ahead, half) in enumerate(SEGMENTS):
            shard = lax.rem(y + ahead, 4)
            parts = []
            for ref in piece_refs:
                length = ref.shape[0] // 8
                first = pl.multiple_of((shard * 2 + half) * length, length)
                parts.append(ref[pl.ds(first, length), :])
            value = parts[0] if count == 1 else jnp.concatenate(parts, axis=0)
            hi = value.astype(BF16)
            panel[index * seg : (index + 1) * seg, :] = hi
            panel[total + index * seg : total + (index + 1) * seg, :] = (
                value - hi.astype(F32)
            ).astype(BF16)
        for q in range(2):
            hi_ref, lo_ref = factor_refs[2 * q : 2 * q + 2]
            for step in range(rows // tile):
                here = slice(step * tile, (step + 1) * tile)
                both = lax.dot_general(panel[...], hi_ref[here, :], NT, preferred_element_type=F32)
                rest = lax.dot_general(
                    panel[:total, :], lo_ref[here, :], NT, preferred_element_type=F32
                )
                value = both[:total] + (both[total:] + rest)
                columns = slice(q * rows + step * tile, q * rows + (step + 1) * tile)
                first = 0
                for ref, size in zip(out_refs, GROUPS):
                    ref[:, columns] = value[first * seg : (first + size) * seg]
                    first += size

    return pl.pallas_call(
        kernel,
        out_shape=[shape_of(size * seg, 2 * rows) for size in GROUPS],
        in_specs=[SMEM] + [VMEM] * (count + 4) + [ANY] * len(earlier),
        out_specs=[VMEM] * 5,
        scratch_shapes=[pltpu.VMEM((2 * total, depth), BF16)],
        compiler_params=params(16),
        cost_estimate=pl.CostEstimate(
            flops=6 * total * 2 * rows * depth, bytes_accessed=8 * rows * depth, transcendentals=0
        ),
        name="fitted",
    )(
        place,
        *pieces,
        *[pltpu.with_memory_space_constraint(factor, pltpu.VMEM) for factor in factors],
        *earlier,
    )


def messages(first, late, earlier):
    size = late[0].shape[0]
    above = first[0].shape[0] if first else 0
    columns = late[0].shape[1]

    def kernel(*refs):
        out_refs = refs[-2:]
        for index, out_ref in enumerate(out_refs):
            if first:
                out_ref[:above, :] = refs[index][...]
            segment_ref, arrived_ref = refs[len(first) + 2 * index : len(first) + 2 * index + 2]
            out_ref[above:, :] = segment_ref[...] + arrived_ref[:size, :]

    return pl.pallas_call(
        kernel,
        out_shape=[shape_of(above + size, columns)] * 2,
        in_specs=[VMEM] * (len(first) + 4) + [ANY] * len(earlier),
        out_specs=[VMEM] * 2,
        compiler_params=params(4),
        name="messages",
    )(*first, *late, *earlier)


def shard_sum(terms, earlier=()):
    sizes = [chunk[0][2] for chunk in terms]
    arrays = [term[0] for chunk in terms for term in chunk]
    columns = arrays[0].shape[1]

    def kernel(*refs):
        out_ref = refs[-1]
        first, index = 0, 0
        for chunk, size in zip(terms, sizes):
            value = None
            for _, start, length in chunk:
                part = refs[index][start : start + length, :]
                value = part if value is None else value + part
                index += 1
            out_ref[first : first + size, :] = value
            first += size

    return pl.pallas_call(
        kernel,
        out_shape=shape_of(sum(sizes), columns),
        in_specs=[VMEM] * len(arrays) + [ANY] * len(earlier),
        out_specs=VMEM,
        compiler_params=params(4),
        name="shard",
    )(*arrays, *earlier)


def exchange_partial(place, kept, arrived, scale):
    rows = sum(part.shape[0] for part in kept)
    width = kept[0].shape[1] // 2
    half_width = width // 2
    count = len(kept)
    half = BLK // 2

    def kernel(place_ref, *refs):
        kept_refs, arrived_refs = refs[:count], refs[count : 2 * count]
        send_ref, *out_refs = refs[2 * count : -3]
        full, hi_ref, lo_ref = refs[-3:]
        y, h, core = place_ref[0], place_ref[1], place_ref[2]
        first = 0
        for kept_ref, arrived_ref in zip(kept_refs, arrived_refs):
            size = kept_ref.shape[0]
            value = kept_ref[...] + arrived_ref[...]
            full[first : first + size, :] = value[:, :width]
            full[rows + first : rows + first + size, :] = value[:, width:]
            first += size
        value = full[...]
        hi = value.astype(BF16)
        hi_ref[...] = hi
        lo_ref[...] = (value - hi.astype(F32)).astype(BF16)
        mine = pl.ds(pl.multiple_of(core * half_width, half_width), half_width)
        theirs = pl.ds(pl.multiple_of((1 - core) * half_width, half_width), half_width)
        places = {}
        index = 0
        for ref, size in zip(out_refs, GROUPS):
            for part in range(size):
                places[SEGMENTS[index]] = (ref, part * half, index * half)
                index += 1
        for ahead in (2, 1, 3, 0):
            block = lax.rem(y + ahead, 4) * 2 + h
            left = full[:, pl.ds(pl.multiple_of(block * BLK, BLK), BLK)].T
            left_hi = left.astype(BF16)
            left_lo = (left - left_hi.astype(F32)).astype(BF16)
            for columns, send in ((theirs, True), (mine, False)):
                right_hi, right_lo = hi_ref[:, columns], lo_ref[:, columns]
                value = jnp.dot(left_hi, right_hi, preferred_element_type=F32)
                value += jnp.dot(left_hi, right_lo, preferred_element_type=F32)
                value += jnp.dot(left_lo, right_hi, preferred_element_type=F32)
                value *= scale
                for side in range(2):
                    ref, first, first_send = places[(ahead, side)]
                    part = value[side * half : (side + 1) * half]
                    if send:
                        send_ref[first_send : first_send + half, :] = part
                    else:
                        ref[first : first + half, :] = part

    return pl.pallas_call(
        kernel,
        out_shape=[shape_of(8 * half, half_width)] + [shape_of(size * half, half_width) for size in GROUPS],
        in_specs=[SMEM] + [VMEM] * (2 * count),
        out_specs=[VMEM] * 6,
        scratch_shapes=[
            pltpu.VMEM((2 * rows, width), F32),
            pltpu.VMEM((2 * rows, width), BF16),
            pltpu.VMEM((2 * rows, width), BF16),
        ],
        compiler_params=params(16),
        name="exchange",
    )(place, *kept, *arrived)


def scatter_y(parts):
    plus, minus, plus_late, minus_late, own = parts
    seg = plus_late.shape[0]
    from_below, from_above = move(plus, "y+"), move(minus, "y-")
    late_below = move(plus_late + from_below[:seg], "y+")
    late_above = move(minus_late + from_above[:seg], "y-")
    near = own + jnp.concatenate([from_above[seg:], from_below[seg:]], axis=0)
    return near + jnp.concatenate([late_below, late_above], axis=0)


def body(b_factors, occupied, b_mask, c_mask):
    aux, orb = lax.axis_index("aux"), lax.axis_index("orb")
    core = lax.rem(aux, 2)
    place = jnp.stack([lax.div(orb, 2), lax.rem(orb, 2), core]).astype(jnp.int32)
    naux = lax.axis_size("aux")
    factor = 1.0 / math.sqrt(b_factors.shape[0] * naux * NOCC)
    own_b, own_mask = b_factors[0], b_mask[0].astype(F32)

    other_b, other_mask = move(own_b, "core"), move(own_mask, "core")
    own_a, own_c = transpose_panel(occupied, c_mask)
    left_a, right_a, across_a = move(own_a, "x+"), move(own_a, "x-"), move(own_a, "zl")
    (own_c,) = after([own_c], left_a, right_a, across_a)
    left_c, right_c, across_c = move(own_c, "x+"), move(own_c, "x-"), move(own_c, "zl")
    factors = (*split_factors(own_b, own_mask), *split_factors(other_b, other_mask))

    segs, plus, minus, waits, owns = [], [], [], [], []

    def late_of(k):
        return waits[k][0], plus[k], waits[k][1], minus[k]

    def send(to_plus, to_minus):
        plus.append(move(to_plus, "y+"))
        minus.append(move(to_minus, "y-"))

    def chunk(pieces, before=(), first=()):
        to_plus, to_minus, *wait, own = fitted_chunk(place, pieces, factors, (*before, *owns[-1:]))
        if owns:
            to_plus, to_minus = messages((to_plus, to_minus), late_of(-1), first)
        send(to_plus, to_minus)
        segs.append(sum(piece.shape[0] for piece in pieces) // 8)
        waits.append(wait)
        owns.append(own)

    kept, arrived = [], []

    def share(k, earlier=()):
        seg = segs[k]
        start = 2 * segs[k + 1] if k + 1 < len(segs) else 0
        terms = [
            [(owns[k], 0, seg), (minus[k], seg, seg), (plus[k + 1], start, seg)],
            [(owns[k], seg, seg), (plus[k], seg, seg), (minus[k + 1], start, seg)],
        ]
        kept.append(shard_sum(terms, earlier))
        arrived.append(move(kept[-1], "zh"))

    chunk((own_a, own_c, left_a, right_a, across_a))
    across_a, right_a = after([across_a, right_a], left_c, right_c, across_c, owns[-1])
    left2_a, far_a, right2_a = move(across_a, "x+"), move(right_a, "x-"), move(right_a, "zl")
    chunk((left_c, right_c, across_c))
    across_c, right_c = after([across_c, right_c], left2_a, far_a, right2_a, owns[-1])
    left2_c, far_c, right2_c = move(across_c, "x+"), move(right_c, "x-"), move(right_c, "zl")
    chunk((left2_a, far_a, right2_a))
    left2_a, right2_c = after([left2_a, right2_c], left2_c, far_c, owns[-1])
    far2 = (move(left2_a, "x+"), move(right2_c, "x-"))
    share(0, (left2_c, far_c, right2_c))
    chunk((left2_c, far_c, right2_c), (kept[0],))
    share(1)
    chunk(far2, (kept[1],), (arrived[0], arrived[1]))
    share(2)
    send(*messages((), late_of(-1), (kept[2],)))
    share(3)
    share(4, (kept[3], arrived[2]))
    other, *parts = exchange_partial(place, kept, arrived, factor)
    other = move(other, "core")
    first, summed = 0, []
    for part in parts:
        size = part.shape[0]
        summed.append(part + other[first : first + size])
        first += size
    block = scatter_y(summed)
    for name in ("zl", "xa", "xb"):
        block = block + move(block, name)
    other = move(block, "core")
    low = jnp.where(core == 0, block, other)
    high = jnp.where(core == 0, other, block)
    return jnp.concatenate([low, high], axis=1)


def solution(mesh):
    placed = (P("aux", None, "orb"), P("orb", "aux"), P("aux", None, "orb"), P("orb", "aux"))
    return jax.shard_map(
        body, mesh=mesh, in_specs=placed, out_specs=P("orb", None), check_vma=False
    )
```

```python
import functools
import math

import jax
import jax.numpy as jnp
from jax import lax
from jax.experimental import pallas as pl
from jax.experimental.pallas import tpu as pltpu
from jax.sharding import PartitionSpec as P

BLK = 128
NOCC = 2048
F32 = jnp.float32
BF16 = jnp.bfloat16
MIB = 1024 * 1024
NT = (((1,), (1,)), ((), ()))


def aux_pairs(move):
    pairs = []
    for z in range(2):
        for x in range(4):
            for core in range(2):
                z2, x2, core2 = move(z, x, core)
                pairs.append((z * 8 + x * 2 + core, z2 * 8 + (x2 % 4) * 2 + core2))
    return pairs


def orb_pairs(move):
    pairs = []
    for y in range(4):
        for h in range(2):
            y2, h2 = move(y, h)
            pairs.append((y * 2 + h, (y2 % 4) * 2 + h2))
    return pairs


MOVES = {
    "x+": ("aux", aux_pairs(lambda z, x, c: (z, x + 1, c))),
    "x-": ("aux", aux_pairs(lambda z, x, c: (z, x - 1, c))),
    "xa": ("aux", aux_pairs(lambda z, x, c: (z, x ^ 1, c))),
    "xb": ("aux", aux_pairs(lambda z, x, c: (z, 3 - x, c))),
    "zl": ("aux", aux_pairs(lambda z, x, c: (1 - z, x, c))),
    "core": ("aux", aux_pairs(lambda z, x, c: (z, x, 1 - c))),
    "y+": ("orb", orb_pairs(lambda y, h: (y + 1, h))),
    "y-": ("orb", orb_pairs(lambda y, h: (y - 1, h))),
    "y2": ("orb", orb_pairs(lambda y, h: (y + 2, h))),
    "zh": ("orb", orb_pairs(lambda y, h: (y, 1 - h))),
}


def move(value, name):
    axis, pairs = MOVES[name]
    return lax.ppermute(value, axis, pairs)


def params(mib):
    return pltpu.CompilerParams(vmem_limit_bytes=mib * MIB)


def whole(shape):
    return pl.BlockSpec(shape, lambda *_: tuple(0 for _ in shape))


SMEM = pl.BlockSpec(memory_space=pltpu.SMEM)
VMEM = pl.BlockSpec(memory_space=pltpu.VMEM)
ANY = pl.BlockSpec(memory_space=pl.ANY)


def shape_of(rows, columns):
    return jax.ShapeDtypeStruct((rows, columns), F32)


def after(values, *earlier):
    count = len(values)

    def kernel(*refs):
        del refs

    return pl.pallas_call(
        kernel,
        out_shape=[jax.ShapeDtypeStruct(value.shape, value.dtype) for value in values],
        in_specs=[ANY] * (count + len(earlier)),
        out_specs=[ANY] * count,
        input_output_aliases={index: index for index in range(count)},
        compiler_params=params(1),
        name="after",
    )(*values, *earlier)

SEGMENTS = ((2, 0), (1, 1), (2, 1), (3, 0), (1, 0), (3, 1), (0, 0), (0, 1))
GROUPS = (2, 2, 1, 1, 2)
AHEAD = (1, 3, 2, 0)


def transpose_panel(occupied, c_mask):
    depth, width = occupied.shape
    half = width // 2

    def kernel(mask_ref, c_ref, first_ref, second_ref):
        for k in range(depth // BLK):
            rows = slice(k * BLK, (k + 1) * BLK)
            block = (c_ref[rows, :] * mask_ref[k, 0].astype(F32)).T
            first_ref[:, rows] = block[:half]
            second_ref[:, rows] = block[half:]

    return pl.pallas_call(
        kernel,
        out_shape=[shape_of(half, depth)] * 2,
        in_specs=[SMEM, VMEM],
        out_specs=[VMEM] * 2,
        compiler_params=params(8),
        name="panel",
    )(c_mask, occupied)


def split_factors(factors, mask):
    rows, depth = factors.shape

    def kernel(mask_ref, b_ref, hi_ref, lo_ref, end_ref):
        row = pl.program_id(0)
        end_ref[...] = b_ref[:8, :BLK]
        here = pl.ds(pl.multiple_of(row * BLK, BLK), BLK)
        for k in range(depth // BLK):
            cols = slice(k * BLK, (k + 1) * BLK)
            value = b_ref[:, cols] * mask_ref[row, k]
            hi = value.astype(BF16)
            hi_ref[here, cols] = hi
            lo_ref[here, cols] = (value - hi.astype(F32)).astype(BF16)

    return pl.pallas_call(
        kernel,
        grid=(rows // BLK,),
        out_shape=[pltpu.VMEM((rows, depth), BF16)] * 2 + [shape_of(8, BLK)],
        in_specs=[SMEM, pl.BlockSpec((BLK, depth), lambda i: (i, 0))],
        out_specs=[VMEM, VMEM, whole((8, BLK))],
        compiler_params=params(8),
        name="split",
    )(mask, factors)


def fitted_chunk(place, pieces, factors, earlier):
    rows, depth = factors[0].shape
    total = sum(piece.shape[0] for piece in pieces)
    seg = total // 8
    tile = 256
    count = len(pieces)

    def kernel(place_ref, *refs):
        piece_refs = refs[:count]
        factor_refs = refs[count : count + 4]
        out_refs = refs[-6:-1]
        panel = refs[-1]
        y = place_ref[0]
        for index, (ahead, half) in enumerate(SEGMENTS):
            shard = lax.rem(y + ahead, 4)
            parts = []
            for ref in piece_refs:
                length = ref.shape[0] // 8
                first = pl.multiple_of((shard * 2 + half) * length, length)
                parts.append(ref[pl.ds(first, length), :])
            value = parts[0] if count == 1 else jnp.concatenate(parts, axis=0)
            hi = value.astype(BF16)
            panel[index * seg : (index + 1) * seg, :] = hi
            panel[total + index * seg : total + (index + 1) * seg, :] = (
                value - hi.astype(F32)
            ).astype(BF16)
        for q in range(2):
            hi_ref, lo_ref = factor_refs[2 * q : 2 * q + 2]
            for step in range(rows // tile):
                here = slice(step * tile, (step + 1) * tile)
                both = lax.dot_general(panel[...], hi_ref[here, :], NT, preferred_element_type=F32)
                rest = lax.dot_general(
                    panel[:total, :], lo_ref[here, :], NT, preferred_element_type=F32
                )
                value = both[:total] + (both[total:] + rest)
                columns = slice(q * rows + step * tile, q * rows + (step + 1) * tile)
                first = 0
                for ref, size in zip(out_refs, GROUPS):
                    ref[:, columns] = value[first * seg : (first + size) * seg]
                    first += size

    return pl.pallas_call(
        kernel,
        out_shape=[shape_of(size * seg, 2 * rows) for size in GROUPS],
        in_specs=[SMEM] + [VMEM] * (count + 4) + [ANY] * len(earlier),
        out_specs=[VMEM] * 5,
        scratch_shapes=[pltpu.VMEM((2 * total, depth), BF16)],
        compiler_params=params(16),
        cost_estimate=pl.CostEstimate(
            flops=6 * total * 2 * rows * depth, bytes_accessed=8 * rows * depth, transcendentals=0
        ),
        name="fitted",
    )(
        place,
        *pieces,
        *[pltpu.with_memory_space_constraint(factor, pltpu.VMEM) for factor in factors],
        *earlier,
    )


def messages(first, late, earlier):
    size = late[0].shape[0]
    above = first[0].shape[0] if first else 0
    columns = late[0].shape[1]

    def kernel(*refs):
        out_refs = refs[-2:]
        for index, out_ref in enumerate(out_refs):
            if first:
                out_ref[:above, :] = refs[index][...]
            segment_ref, arrived_ref = refs[len(first) + 2 * index : len(first) + 2 * index + 2]
            out_ref[above:, :] = segment_ref[...] + arrived_ref[:size, :]

    return pl.pallas_call(
        kernel,
        out_shape=[shape_of(above + size, columns)] * 2,
        in_specs=[VMEM] * (len(first) + 4) + [ANY] * len(earlier),
        out_specs=[VMEM] * 2,
        compiler_params=params(4),
        name="messages",
    )(*first, *late, *earlier)


def shard_sum(terms, earlier=()):
    sizes = [chunk[0][2] for chunk in terms]
    arrays = [term[0] for chunk in terms for term in chunk]
    columns = arrays[0].shape[1]

    def kernel(*refs):
        out_ref = refs[-1]
        first, index = 0, 0
        for chunk, size in zip(terms, sizes):
            value = None
            for _, start, length in chunk:
                part = refs[index][start : start + length, :]
                value = part if value is None else value + part
                index += 1
            out_ref[first : first + size, :] = value
            first += size

    return pl.pallas_call(
        kernel,
        out_shape=shape_of(sum(sizes), columns),
        in_specs=[VMEM] * len(arrays) + [ANY] * len(earlier),
        out_specs=VMEM,
        compiler_params=params(4),
        name="shard",
    )(*arrays, *earlier)


def exchange_partial(place, kept, arrived, scale):
    rows = sum(part.shape[0] for part in kept)
    width = kept[0].shape[1] // 2
    half_width = width // 2
    count = len(kept)

    def kernel(place_ref, *refs):
        kept_refs, arrived_refs = refs[:count], refs[count : 2 * count]
        send_ref, *out_refs = refs[2 * count : -3]
        full, hi_ref, lo_ref = refs[-3:]
        y, h, core = place_ref[0], place_ref[1], place_ref[2]
        first = 0
        for kept_ref, arrived_ref in zip(kept_refs, arrived_refs):
            size = kept_ref.shape[0]
            value = kept_ref[...] + arrived_ref[...]
            full[first : first + size, :] = value[:, :width]
            full[rows + first : rows + first + size, :] = value[:, width:]
            first += size
        value = full[...]
        hi = value.astype(BF16)
        hi_ref[...] = hi
        lo_ref[...] = (value - hi.astype(F32)).astype(BF16)
        mine = pl.ds(pl.multiple_of(core * half_width, half_width), half_width)
        theirs = pl.ds(pl.multiple_of((1 - core) * half_width, half_width), half_width)
        for index, ahead in enumerate(AHEAD):
            block = lax.rem(y + ahead, 4) * 2 + h
            left = full[:, pl.ds(pl.multiple_of(block * BLK, BLK), BLK)].T
            left_hi = left.astype(BF16)
            left_lo = (left - left_hi.astype(F32)).astype(BF16)
            for columns, send in ((theirs, True), (mine, False)):
                right_hi, right_lo = hi_ref[:, columns], lo_ref[:, columns]
                value = jnp.dot(left_hi, right_hi, preferred_element_type=F32)
                value += jnp.dot(left_hi, right_lo, preferred_element_type=F32)
                value += jnp.dot(left_lo, right_hi, preferred_element_type=F32)
                value *= scale
                if send:
                    send_ref[index * BLK : (index + 1) * BLK, :] = value
                else:
                    out_refs[index][...] = value

    return pl.pallas_call(
        kernel,
        out_shape=[shape_of(4 * BLK, half_width)] + [shape_of(BLK, half_width)] * 4,
        in_specs=[SMEM] + [VMEM] * (2 * count),
        out_specs=[VMEM] * 5,
        scratch_shapes=[
            pltpu.VMEM((2 * rows, width), F32),
            pltpu.VMEM((2 * rows, width), BF16),
            pltpu.VMEM((2 * rows, width), BF16),
        ],
        compiler_params=params(16),
        name="exchange",
    )(place, *kept, *arrived)


def body(b_factors, occupied, b_mask, c_mask):
    aux, orb = lax.axis_index("aux"), lax.axis_index("orb")
    core = lax.rem(aux, 2)
    place = jnp.stack([lax.div(orb, 2), lax.rem(orb, 2), core]).astype(jnp.int32)
    naux = lax.axis_size("aux")
    factor = 1.0 / math.sqrt(b_factors.shape[0] * naux * NOCC)
    own_b, own_mask = b_factors[0], b_mask[0].astype(F32)

    other_b, other_mask = move(own_b, "core"), move(own_mask, "core")
    own_a, own_c = transpose_panel(occupied, c_mask)
    left_a, right_a, across_a = move(own_a, "x+"), move(own_a, "x-"), move(own_a, "zl")
    own_hi, own_lo, _ = split_factors(own_b, own_mask)
    other_hi, other_lo, end = split_factors(other_b, other_mask)
    factors = (own_hi, own_lo, other_hi, other_lo)
    (own_c,) = after([own_c], left_a, right_a, across_a, end)
    left_c, right_c, across_c = move(own_c, "x+"), move(own_c, "x-"), move(own_c, "zl")

    segs, plus, minus, waits, owns = [], [], [], [], []

    def late_of(k):
        return waits[k][0], plus[k], waits[k][1], minus[k]

    def send(to_plus, to_minus):
        plus.append(move(to_plus, "y+"))
        minus.append(move(to_minus, "y-"))

    def chunk(pieces, before=(), first=()):
        to_plus, to_minus, *wait, own = fitted_chunk(place, pieces, factors, (*before, *owns[-1:]))
        if owns:
            to_plus, to_minus = messages((to_plus, to_minus), late_of(-1), first)
        send(to_plus, to_minus)
        segs.append(sum(piece.shape[0] for piece in pieces) // 8)
        waits.append(wait)
        owns.append(own)

    kept, arrived = [], []

    def share(k, earlier=()):
        seg = segs[k]
        start = 2 * segs[k + 1] if k + 1 < len(segs) else 0
        terms = [
            [(owns[k], 0, seg), (minus[k], seg, seg), (plus[k + 1], start, seg)],
            [(owns[k], seg, seg), (plus[k], seg, seg), (minus[k + 1], start, seg)],
        ]
        kept.append(shard_sum(terms, earlier))
        arrived.append(move(kept[-1], "zh"))

    chunk((own_a, own_c, left_a, right_a, across_a))
    across_a, right_a = after([across_a, right_a], left_c, right_c, across_c, owns[-1])
    left2_a, far_a, right2_a = move(across_a, "x+"), move(right_a, "x-"), move(right_a, "zl")
    chunk((left_c, right_c, across_c))
    across_c, right_c = after([across_c, right_c], left2_a, far_a, right2_a, owns[-1])
    left2_c, far_c, right2_c = move(across_c, "x+"), move(right_c, "x-"), move(right_c, "zl")
    chunk((left2_a, far_a, right2_a))
    left2_a, right2_c = after([left2_a, right2_c], left2_c, far_c, owns[-1])
    far2 = (move(left2_a, "x+"), move(right2_c, "x-"))
    share(0, (left2_c, far_c, right2_c))
    chunk((left2_c, far_c, right2_c), (kept[0],))
    share(1)
    chunk(far2, (kept[1],), (arrived[0], arrived[1]))
    share(2)
    send(*messages((), late_of(-1), (kept[2],)))
    share(3)
    share(4, (kept[3], arrived[2]))
    other, *parts = exchange_partial(place, kept, arrived, factor)
    other = move(other, "core")
    parts = [part + other[k * BLK : (k + 1) * BLK] for k, part in enumerate(parts)]
    block = parts[-1]
    for part in [move(part, name) for part, name in zip(parts, ("y+", "y-", "y2"))]:
        block = block + part
    for name in ("zl", "xa", "xb"):
        block = block + move(block, name)
    other = move(block, "core")
    low = jnp.where(core == 0, block, other)
    high = jnp.where(core == 0, other, block)
    return jnp.concatenate([low, high], axis=1)


def solution(mesh):
    placed = (P("aux", None, "orb"), P("orb", "aux"), P("aux", None, "orb"), P("orb", "aux"))
    return jax.shard_map(
        body, mesh=mesh, in_specs=placed, out_specs=P("orb", None), check_vma=False
    )
```

```python
import functools
import math

import jax
import jax.numpy as jnp
from jax import lax
from jax.experimental import pallas as pl
from jax.experimental.pallas import tpu as pltpu
from jax.sharding import PartitionSpec as P

BLK = 128
NOCC = 2048
F32 = jnp.float32
BF16 = jnp.bfloat16
MIB = 1024 * 1024
NT = (((1,), (1,)), ((), ()))


def aux_pairs(move):
    pairs = []
    for z in range(2):
        for x in range(4):
            for core in range(2):
                z2, x2, core2 = move(z, x, core)
                pairs.append((z * 8 + x * 2 + core, z2 * 8 + (x2 % 4) * 2 + core2))
    return pairs


def orb_pairs(move):
    pairs = []
    for y in range(4):
        for h in range(2):
            y2, h2 = move(y, h)
            pairs.append((y * 2 + h, (y2 % 4) * 2 + h2))
    return pairs


MOVES = {
    "x+": ("aux", aux_pairs(lambda z, x, c: (z, x + 1, c))),
    "x-": ("aux", aux_pairs(lambda z, x, c: (z, x - 1, c))),
    "xa": ("aux", aux_pairs(lambda z, x, c: (z, x ^ 1, c))),
    "xb": ("aux", aux_pairs(lambda z, x, c: (z, 3 - x, c))),
    "zl": ("aux", aux_pairs(lambda z, x, c: (1 - z, x, c))),
    "core": ("aux", aux_pairs(lambda z, x, c: (z, x, 1 - c))),
    "y+": ("orb", orb_pairs(lambda y, h: (y + 1, h))),
    "y-": ("orb", orb_pairs(lambda y, h: (y - 1, h))),
    "y2": ("orb", orb_pairs(lambda y, h: (y + 2, h))),
    "zh": ("orb", orb_pairs(lambda y, h: (y, 1 - h))),
}


def move(value, name):
    axis, pairs = MOVES[name]
    return lax.ppermute(value, axis, pairs)


def params(mib):
    return pltpu.CompilerParams(vmem_limit_bytes=mib * MIB)


def whole(shape):
    return pl.BlockSpec(shape, lambda *_: tuple(0 for _ in shape))


SMEM = pl.BlockSpec(memory_space=pltpu.SMEM)
VMEM = pl.BlockSpec(memory_space=pltpu.VMEM)
ANY = pl.BlockSpec(memory_space=pl.ANY)


def shape_of(rows, columns):
    return jax.ShapeDtypeStruct((rows, columns), F32)


def after(values, *earlier):
    count = len(values)

    def kernel(*refs):
        del refs

    return pl.pallas_call(
        kernel,
        out_shape=[jax.ShapeDtypeStruct(value.shape, value.dtype) for value in values],
        in_specs=[ANY] * (count + len(earlier)),
        out_specs=[ANY] * count,
        input_output_aliases={index: index for index in range(count)},
        compiler_params=params(1),
        name="after",
    )(*values, *earlier)

SEGMENTS = ((2, 0), (1, 1), (2, 1), (3, 0), (1, 0), (3, 1), (0, 0), (0, 1))
GROUPS = (2, 2, 1, 1, 2)
AHEAD = (1, 3, 2, 0)


def transpose_panel(occupied, c_mask):
    depth, width = occupied.shape
    half = width // 2

    def kernel(mask_ref, c_ref, first_ref, second_ref):
        for k in range(depth // BLK):
            rows = slice(k * BLK, (k + 1) * BLK)
            block = (c_ref[rows, :] * mask_ref[k, 0].astype(F32)).T
            first_ref[:, rows] = block[:half]
            second_ref[:, rows] = block[half:]

    return pl.pallas_call(
        kernel,
        out_shape=[shape_of(half, depth)] * 2,
        in_specs=[SMEM, VMEM],
        out_specs=[VMEM] * 2,
        compiler_params=params(8),
        name="panel",
    )(c_mask, occupied)


def split_factors(factors, mask):
    rows, depth = factors.shape

    def kernel(mask_ref, b_ref, hi_ref, lo_ref, end_ref):
        row = pl.program_id(0)
        end_ref[...] = b_ref[:8, :BLK]
        here = pl.ds(pl.multiple_of(row * BLK, BLK), BLK)
        for k in range(depth // BLK):
            cols = slice(k * BLK, (k + 1) * BLK)
            value = b_ref[:, cols] * mask_ref[row, k]
            hi = value.astype(BF16)
            hi_ref[here, cols] = hi
            lo_ref[here, cols] = (value - hi.astype(F32)).astype(BF16)

    return pl.pallas_call(
        kernel,
        grid=(rows // BLK,),
        out_shape=[pltpu.VMEM((rows, depth), BF16)] * 2 + [shape_of(8, BLK)],
        in_specs=[SMEM, pl.BlockSpec((BLK, depth), lambda i: (i, 0))],
        out_specs=[VMEM, VMEM, whole((8, BLK))],
        compiler_params=params(8),
        name="split",
    )(mask, factors)


def fitted_chunk(place, pieces, factors, earlier):
    rows, depth = factors[0].shape
    total = sum(piece.shape[0] for piece in pieces)
    seg = total // 8
    tile = 256
    count = len(pieces)

    def kernel(place_ref, *refs):
        piece_refs = refs[:count]
        factor_refs = refs[count : count + 4]
        out_refs = refs[-6:-1]
        panel = refs[-1]
        y = place_ref[0]
        for index, (ahead, half) in enumerate(SEGMENTS):
            shard = lax.rem(y + ahead, 4)
            parts = []
            for ref in piece_refs:
                length = ref.shape[0] // 8
                first = pl.multiple_of((shard * 2 + half) * length, length)
                parts.append(ref[pl.ds(first, length), :])
            value = parts[0] if count == 1 else jnp.concatenate(parts, axis=0)
            hi = value.astype(BF16)
            panel[index * seg : (index + 1) * seg, :] = hi
            panel[total + index * seg : total + (index + 1) * seg, :] = (
                value - hi.astype(F32)
            ).astype(BF16)
        for q in range(2):
            hi_ref, lo_ref = factor_refs[2 * q : 2 * q + 2]
            for step in range(rows // tile):
                here = slice(step * tile, (step + 1) * tile)
                both = lax.dot_general(panel[...], hi_ref[here, :], NT, preferred_element_type=F32)
                rest = lax.dot_general(
                    panel[:total, :], lo_ref[here, :], NT, preferred_element_type=F32
                )
                value = both[:total] + (both[total:] + rest)
                columns = slice(q * rows + step * tile, q * rows + (step + 1) * tile)
                first = 0
                for ref, size in zip(out_refs, GROUPS):
                    ref[:, columns] = value[first * seg : (first + size) * seg]
                    first += size

    return pl.pallas_call(
        kernel,
        out_shape=[shape_of(size * seg, 2 * rows) for size in GROUPS],
        in_specs=[SMEM] + [VMEM] * (count + 4) + [ANY] * len(earlier),
        out_specs=[VMEM] * 5,
        scratch_shapes=[pltpu.VMEM((2 * total, depth), BF16)],
        compiler_params=params(16),
        cost_estimate=pl.CostEstimate(
            flops=6 * total * 2 * rows * depth, bytes_accessed=8 * rows * depth, transcendentals=0
        ),
        name="fitted",
    )(
        place,
        *pieces,
        *[pltpu.with_memory_space_constraint(factor, pltpu.VMEM) for factor in factors],
        *earlier,
    )


def messages(first, late, earlier):
    size = late[0].shape[0]
    above = first[0].shape[0] if first else 0
    columns = late[0].shape[1]

    def kernel(*refs):
        out_refs = refs[-2:]
        for index, out_ref in enumerate(out_refs):
            if first:
                out_ref[:above, :] = refs[index][...]
            segment_ref, arrived_ref = refs[len(first) + 2 * index : len(first) + 2 * index + 2]
            out_ref[above:, :] = segment_ref[...] + arrived_ref[:size, :]

    return pl.pallas_call(
        kernel,
        out_shape=[shape_of(above + size, columns)] * 2,
        in_specs=[VMEM] * (len(first) + 4) + [ANY] * len(earlier),
        out_specs=[VMEM] * 2,
        compiler_params=params(4),
        name="messages",
    )(*first, *late, *earlier)


def shard_sum(terms, earlier=()):
    sizes = [chunk[0][2] for chunk in terms]
    arrays = [term[0] for chunk in terms for term in chunk]
    columns = arrays[0].shape[1]

    def kernel(*refs):
        out_ref = refs[-1]
        first, index = 0, 0
        for chunk, size in zip(terms, sizes):
            value = None
            for _, start, length in chunk:
                part = refs[index][start : start + length, :]
                value = part if value is None else value + part
                index += 1
            out_ref[first : first + size, :] = value
            first += size

    return pl.pallas_call(
        kernel,
        out_shape=shape_of(sum(sizes), columns),
        in_specs=[VMEM] * len(arrays) + [ANY] * len(earlier),
        out_specs=VMEM,
        compiler_params=params(4),
        name="shard",
    )(*arrays, *earlier)


def exchange_partial(place, kept, arrived, scale, base):
    rows = sum(part.shape[0] for part in kept)
    width = kept[0].shape[1] // 2
    half_width = width // 2
    count = len(kept)

    def kernel(place_ref, *refs):
        kept_refs, arrived_refs = refs[:count], refs[count : 2 * count]
        base_refs = refs[2 * count : -8]
        send_ref, *out_refs = refs[-8:-3]
        full, hi_ref, lo_ref = refs[-3:]
        y, h, core = place_ref[0], place_ref[1], place_ref[2]
        first = 0
        for kept_ref, arrived_ref in zip(kept_refs, arrived_refs):
            size = kept_ref.shape[0]
            value = kept_ref[...] + arrived_ref[...]
            full[first : first + size, :] = value[:, :width]
            full[rows + first : rows + first + size, :] = value[:, width:]
            first += size
        value = full[...]
        hi = value.astype(BF16)
        hi_ref[...] = hi
        lo_ref[...] = (value - hi.astype(F32)).astype(BF16)
        mine = pl.ds(pl.multiple_of(core * half_width, half_width), half_width)
        theirs = pl.ds(pl.multiple_of((1 - core) * half_width, half_width), half_width)
        for index, ahead in enumerate(AHEAD):
            block = lax.rem(y + ahead, 4) * 2 + h
            left = full[:, pl.ds(pl.multiple_of(block * BLK, BLK), BLK)].T
            left_hi = left.astype(BF16)
            left_lo = (left - left_hi.astype(F32)).astype(BF16)
            for columns, send in ((theirs, True), (mine, False)):
                right_hi, right_lo = hi_ref[:, columns], lo_ref[:, columns]
                value = jnp.dot(left_hi, right_hi, preferred_element_type=F32)
                value += jnp.dot(left_hi, right_lo, preferred_element_type=F32)
                value += jnp.dot(left_lo, right_hi, preferred_element_type=F32)
                value *= scale
                rows_here = slice(index * BLK, (index + 1) * BLK)
                if send:
                    send_ref[rows_here, :] = value + base_refs[0][rows_here, :] if base else value
                else:
                    out_refs[index][...] = value + base_refs[index + 1][...] if base else value

    return pl.pallas_call(
        kernel,
        out_shape=[shape_of(4 * BLK, half_width)] + [shape_of(BLK, half_width)] * 4,
        in_specs=[SMEM] + [VMEM] * (2 * count + len(base)),
        out_specs=[VMEM] * 5,
        scratch_shapes=[
            pltpu.VMEM((2 * rows, width), F32),
            pltpu.VMEM((2 * rows, width), BF16),
            pltpu.VMEM((2 * rows, width), BF16),
        ],
        compiler_params=params(16),
        name="exchange",
    )(place, *kept, *arrived, *base)


def body(b_factors, occupied, b_mask, c_mask):
    aux, orb = lax.axis_index("aux"), lax.axis_index("orb")
    core = lax.rem(aux, 2)
    place = jnp.stack([lax.div(orb, 2), lax.rem(orb, 2), core]).astype(jnp.int32)
    naux = lax.axis_size("aux")
    factor = 1.0 / math.sqrt(b_factors.shape[0] * naux * NOCC)
    own_b, own_mask = b_factors[0], b_mask[0].astype(F32)

    other_b, other_mask = move(own_b, "core"), move(own_mask, "core")
    own_a, own_c = transpose_panel(occupied, c_mask)
    left_a, right_a, across_a = move(own_a, "x+"), move(own_a, "x-"), move(own_a, "zl")
    own_hi, own_lo, _ = split_factors(own_b, own_mask)
    other_hi, other_lo, end = split_factors(other_b, other_mask)
    factors = (own_hi, own_lo, other_hi, other_lo)
    (own_c,) = after([own_c], left_a, right_a, across_a, end)
    left_c, right_c, across_c = move(own_c, "x+"), move(own_c, "x-"), move(own_c, "zl")

    segs, plus, minus, waits, owns = [], [], [], [], []

    def late_of(k):
        return waits[k][0], plus[k], waits[k][1], minus[k]

    def send(to_plus, to_minus):
        plus.append(move(to_plus, "y+"))
        minus.append(move(to_minus, "y-"))

    def chunk(pieces, before=(), first=()):
        to_plus, to_minus, *wait, own = fitted_chunk(place, pieces, factors, (*before, *owns[-1:]))
        if owns:
            to_plus, to_minus = messages((to_plus, to_minus), late_of(-1), first)
        send(to_plus, to_minus)
        segs.append(sum(piece.shape[0] for piece in pieces) // 8)
        waits.append(wait)
        owns.append(own)

    kept, arrived = [], []

    def share(k, earlier=()):
        seg = segs[k]
        start = 2 * segs[k + 1] if k + 1 < len(segs) else 0
        terms = [
            [(owns[k], 0, seg), (minus[k], seg, seg), (plus[k + 1], start, seg)],
            [(owns[k], seg, seg), (plus[k], seg, seg), (minus[k + 1], start, seg)],
        ]
        kept.append(shard_sum(terms, earlier))
        arrived.append(move(kept[-1], "zh"))

    chunk((own_a, own_c, left_a, right_a, across_a))
    across_a, right_a = after([across_a, right_a], left_c, right_c, across_c, owns[-1])
    left2_a, far_a, right2_a = move(across_a, "x+"), move(right_a, "x-"), move(right_a, "zl")
    chunk((left_c, right_c, across_c))
    across_c, right_c = after([across_c, right_c], left2_a, far_a, right2_a, owns[-1])
    left2_c, far_c, right2_c = move(across_c, "x+"), move(right_c, "x-"), move(right_c, "zl")
    chunk((left2_a, far_a, right2_a))
    left2_a, right2_c = after([left2_a, right2_c], left2_c, far_c, owns[-1])
    far2 = (move(left2_a, "x+"), move(right2_c, "x-"))
    share(0, (left2_c, far_c, right2_c))
    chunk((left2_c, far_c, right2_c), (kept[0],))
    share(1)
    chunk(far2, (kept[1],), (arrived[0], arrived[1]))
    share(2)
    send(*messages((), late_of(-1), (kept[2],)))
    share(3)
    share(4, (kept[3], arrived[2]))
    base = exchange_partial(place, kept[:2], arrived[:2], factor, ())
    other, *parts = exchange_partial(place, kept[2:], arrived[2:], factor, base)
    other = move(other, "core")
    parts = [part + other[k * BLK : (k + 1) * BLK] for k, part in enumerate(parts)]
    block = parts[-1]
    for part in [move(part, name) for part, name in zip(parts, ("y+", "y-", "y2"))]:
        block = block + part
    for name in ("zl", "xa", "xb"):
        block = block + move(block, name)
    other = move(block, "core")
    low = jnp.where(core == 0, block, other)
    high = jnp.where(core == 0, other, block)
    return jnp.concatenate([low, high], axis=1)


def solution(mesh):
    placed = (P("aux", None, "orb"), P("orb", "aux"), P("aux", None, "orb"), P("orb", "aux"))
    return jax.shard_map(
        body, mesh=mesh, in_specs=placed, out_specs=P("orb", None), check_vma=False
    )
```

```python
import functools
import math

import jax
import jax.numpy as jnp
from jax import lax
from jax.experimental import pallas as pl
from jax.experimental.pallas import tpu as pltpu
from jax.sharding import PartitionSpec as P

BLK = 128
NOCC = 2048
F32 = jnp.float32
BF16 = jnp.bfloat16
MIB = 1024 * 1024
NT = (((1,), (1,)), ((), ()))


def aux_pairs(move):
    pairs = []
    for z in range(2):
        for x in range(4):
            for core in range(2):
                z2, x2, core2 = move(z, x, core)
                pairs.append((z * 8 + x * 2 + core, z2 * 8 + (x2 % 4) * 2 + core2))
    return pairs


def orb_pairs(move):
    pairs = []
    for y in range(4):
        for h in range(2):
            y2, h2 = move(y, h)
            pairs.append((y * 2 + h, (y2 % 4) * 2 + h2))
    return pairs


MOVES = {
    "x+": ("aux", aux_pairs(lambda z, x, c: (z, x + 1, c))),
    "x-": ("aux", aux_pairs(lambda z, x, c: (z, x - 1, c))),
    "xa": ("aux", aux_pairs(lambda z, x, c: (z, x ^ 1, c))),
    "xb": ("aux", aux_pairs(lambda z, x, c: (z, 3 - x, c))),
    "zl": ("aux", aux_pairs(lambda z, x, c: (1 - z, x, c))),
    "core": ("aux", aux_pairs(lambda z, x, c: (z, x, 1 - c))),
    "y+": ("orb", orb_pairs(lambda y, h: (y + 1, h))),
    "y-": ("orb", orb_pairs(lambda y, h: (y - 1, h))),
    "y2": ("orb", orb_pairs(lambda y, h: (y + 2, h))),
    "zh": ("orb", orb_pairs(lambda y, h: (y, 1 - h))),
}


def move(value, name):
    axis, pairs = MOVES[name]
    return lax.ppermute(value, axis, pairs)


def params(mib):
    return pltpu.CompilerParams(vmem_limit_bytes=mib * MIB)


def whole(shape):
    return pl.BlockSpec(shape, lambda *_: tuple(0 for _ in shape))


SMEM = pl.BlockSpec(memory_space=pltpu.SMEM)
VMEM = pl.BlockSpec(memory_space=pltpu.VMEM)
ANY = pl.BlockSpec(memory_space=pl.ANY)


def shape_of(rows, columns):
    return jax.ShapeDtypeStruct((rows, columns), F32)


def after(values, *earlier):
    count = len(values)

    def kernel(*refs):
        del refs

    return pl.pallas_call(
        kernel,
        out_shape=[jax.ShapeDtypeStruct(value.shape, value.dtype) for value in values],
        in_specs=[ANY] * (count + len(earlier)),
        out_specs=[ANY] * count,
        input_output_aliases={index: index for index in range(count)},
        compiler_params=params(1),
        name="after",
    )(*values, *earlier)

SEGMENTS = ((2, 0), (1, 1), (2, 1), (3, 0), (1, 0), (3, 1), (0, 0), (0, 1))
GROUPS = (2, 2, 1, 1, 2)
AHEAD = (1, 3, 2, 0)


def transpose_panel(occupied, c_mask):
    depth, width = occupied.shape
    half = width // 2

    def kernel(mask_ref, c_ref, first_ref, second_ref):
        for k in range(depth // BLK):
            rows = slice(k * BLK, (k + 1) * BLK)
            block = (c_ref[rows, :] * mask_ref[k, 0].astype(F32)).T
            first_ref[:, rows] = block[:half]
            second_ref[:, rows] = block[half:]

    return pl.pallas_call(
        kernel,
        out_shape=[shape_of(half, depth)] * 2,
        in_specs=[SMEM, VMEM],
        out_specs=[VMEM] * 2,
        compiler_params=params(8),
        name="panel",
    )(c_mask, occupied)


def split_factors(factors, mask):
    rows, depth = factors.shape

    def kernel(mask_ref, b_ref, hi_ref, lo_ref, end_ref):
        row = pl.program_id(0)
        end_ref[...] = b_ref[:8, :BLK]
        here = pl.ds(pl.multiple_of(row * BLK, BLK), BLK)
        for k in range(depth // BLK):
            cols = slice(k * BLK, (k + 1) * BLK)
            value = b_ref[:, cols] * mask_ref[row, k]
            hi = value.astype(BF16)
            hi_ref[here, cols] = hi
            lo_ref[here, cols] = (value - hi.astype(F32)).astype(BF16)

    return pl.pallas_call(
        kernel,
        grid=(rows // BLK,),
        out_shape=[pltpu.VMEM((rows, depth), BF16)] * 2 + [shape_of(8, BLK)],
        in_specs=[SMEM, pl.BlockSpec((BLK, depth), lambda i: (i, 0))],
        out_specs=[VMEM, VMEM, whole((8, BLK))],
        compiler_params=params(8),
        name="split",
    )(mask, factors)


def fitted_chunk(place, pieces, factors, earlier):
    rows, depth = factors[0].shape
    total = sum(piece.shape[0] for piece in pieces)
    seg = total // 8
    tile = 256
    count = len(pieces)

    def kernel(place_ref, *refs):
        piece_refs = refs[:count]
        factor_refs = refs[count : count + 4]
        out_refs = refs[-7:-2]
        full, panel = refs[-2:]
        y = place_ref[0]
        for index, (ahead, half) in enumerate(SEGMENTS):
            shard = lax.rem(y + ahead, 4)
            parts = []
            for ref in piece_refs:
                length = ref.shape[0] // 8
                first = pl.multiple_of((shard * 2 + half) * length, length)
                parts.append(ref[pl.ds(first, length), :])
            value = parts[0] if count == 1 else jnp.concatenate(parts, axis=0)
            full[index * seg : (index + 1) * seg, :] = value
        for first in range(0, total, 64):
            value = full[first : first + 64, :]
            hi = value.astype(BF16)
            panel[first : first + 64, :] = hi
            panel[total + first : total + first + 64, :] = (value - hi.astype(F32)).astype(BF16)
        for q in range(2):
            hi_ref, lo_ref = factor_refs[2 * q : 2 * q + 2]
            for step in range(rows // tile):
                here = slice(step * tile, (step + 1) * tile)
                both = lax.dot_general(panel[...], hi_ref[here, :], NT, preferred_element_type=F32)
                rest = lax.dot_general(
                    panel[:total, :], lo_ref[here, :], NT, preferred_element_type=F32
                )
                value = both[:total] + (both[total:] + rest)
                columns = slice(q * rows + step * tile, q * rows + (step + 1) * tile)
                first = 0
                for ref, size in zip(out_refs, GROUPS):
                    ref[:, columns] = value[first * seg : (first + size) * seg]
                    first += size

    return pl.pallas_call(
        kernel,
        out_shape=[shape_of(size * seg, 2 * rows) for size in GROUPS],
        in_specs=[SMEM] + [VMEM] * (count + 4) + [ANY] * len(earlier),
        out_specs=[VMEM] * 5,
        scratch_shapes=[pltpu.VMEM((total, depth), F32), pltpu.VMEM((2 * total, depth), BF16)],
        compiler_params=params(16),
        cost_estimate=pl.CostEstimate(
            flops=6 * total * 2 * rows * depth, bytes_accessed=8 * rows * depth, transcendentals=0
        ),
        name="fitted",
    )(
        place,
        *pieces,
        *[pltpu.with_memory_space_constraint(factor, pltpu.VMEM) for factor in factors],
        *earlier,
    )


def messages(first, late, earlier):
    size = late[0].shape[0]
    above = first[0].shape[0] if first else 0
    columns = late[0].shape[1]

    def kernel(*refs):
        out_refs = refs[-2:]
        for index, out_ref in enumerate(out_refs):
            if first:
                out_ref[:above, :] = refs[index][...]
            segment_ref, arrived_ref = refs[len(first) + 2 * index : len(first) + 2 * index + 2]
            out_ref[above:, :] = segment_ref[...] + arrived_ref[:size, :]

    return pl.pallas_call(
        kernel,
        out_shape=[shape_of(above + size, columns)] * 2,
        in_specs=[VMEM] * (len(first) + 4) + [ANY] * len(earlier),
        out_specs=[VMEM] * 2,
        compiler_params=params(4),
        name="messages",
    )(*first, *late, *earlier)


def shard_sum(terms, earlier=()):
    sizes = [chunk[0][2] for chunk in terms]
    arrays = [term[0] for chunk in terms for term in chunk]
    columns = arrays[0].shape[1]

    def kernel(*refs):
        out_ref = refs[-1]
        first, index = 0, 0
        for chunk, size in zip(terms, sizes):
            value = None
            for _, start, length in chunk:
                part = refs[index][start : start + length, :]
                value = part if value is None else value + part
                index += 1
            out_ref[first : first + size, :] = value
            first += size

    return pl.pallas_call(
        kernel,
        out_shape=shape_of(sum(sizes), columns),
        in_specs=[VMEM] * len(arrays) + [ANY] * len(earlier),
        out_specs=VMEM,
        compiler_params=params(4),
        name="shard",
    )(*arrays, *earlier)


def exchange_partial(place, kept, arrived, scale, base):
    rows = sum(part.shape[0] for part in kept)
    width = kept[0].shape[1] // 2
    half_width = width // 2
    count = len(kept)

    def kernel(place_ref, *refs):
        kept_refs, arrived_refs = refs[:count], refs[count : 2 * count]
        base_refs = refs[2 * count : -8]
        send_ref, *out_refs = refs[-8:-3]
        full, hi_ref, lo_ref = refs[-3:]
        y, h, core = place_ref[0], place_ref[1], place_ref[2]
        first = 0
        for kept_ref, arrived_ref in zip(kept_refs, arrived_refs):
            size = kept_ref.shape[0]
            value = kept_ref[...] + arrived_ref[...]
            full[first : first + size, :] = value[:, :width]
            full[rows + first : rows + first + size, :] = value[:, width:]
            first += size
        value = full[...]
        hi = value.astype(BF16)
        hi_ref[...] = hi
        lo_ref[...] = (value - hi.astype(F32)).astype(BF16)
        mine = pl.ds(pl.multiple_of(core * half_width, half_width), half_width)
        theirs = pl.ds(pl.multiple_of((1 - core) * half_width, half_width), half_width)
        for index, ahead in enumerate(AHEAD):
            block = lax.rem(y + ahead, 4) * 2 + h
            left = full[:, pl.ds(pl.multiple_of(block * BLK, BLK), BLK)].T
            left_hi = left.astype(BF16)
            left_lo = (left - left_hi.astype(F32)).astype(BF16)
            for columns, send in ((theirs, True), (mine, False)):
                right_hi, right_lo = hi_ref[:, columns], lo_ref[:, columns]
                value = jnp.dot(left_hi, right_hi, preferred_element_type=F32)
                value += jnp.dot(left_hi, right_lo, preferred_element_type=F32)
                value += jnp.dot(left_lo, right_hi, preferred_element_type=F32)
                value *= scale
                rows_here = slice(index * BLK, (index + 1) * BLK)
                if send:
                    send_ref[rows_here, :] = value + base_refs[0][rows_here, :] if base else value
                else:
                    out_refs[index][...] = value + base_refs[index + 1][...] if base else value

    return pl.pallas_call(
        kernel,
        out_shape=[shape_of(4 * BLK, half_width)] + [shape_of(BLK, half_width)] * 4,
        in_specs=[SMEM] + [VMEM] * (2 * count + len(base)),
        out_specs=[VMEM] * 5,
        scratch_shapes=[
            pltpu.VMEM((2 * rows, width), F32),
            pltpu.VMEM((2 * rows, width), BF16),
            pltpu.VMEM((2 * rows, width), BF16),
        ],
        compiler_params=params(16),
        name="exchange",
    )(place, *kept, *arrived, *base)


def body(b_factors, occupied, b_mask, c_mask):
    aux, orb = lax.axis_index("aux"), lax.axis_index("orb")
    core = lax.rem(aux, 2)
    place = jnp.stack([lax.div(orb, 2), lax.rem(orb, 2), core]).astype(jnp.int32)
    naux = lax.axis_size("aux")
    factor = 1.0 / math.sqrt(b_factors.shape[0] * naux * NOCC)
    own_b, own_mask = b_factors[0], b_mask[0].astype(F32)

    other_b, other_mask = move(own_b, "core"), move(own_mask, "core")
    own_a, own_c = transpose_panel(occupied, c_mask)
    left_a, right_a, across_a = move(own_a, "x+"), move(own_a, "x-"), move(own_a, "zl")
    own_hi, own_lo, _ = split_factors(own_b, own_mask)
    other_hi, other_lo, end = split_factors(other_b, other_mask)
    factors = (own_hi, own_lo, other_hi, other_lo)
    (own_c,) = after([own_c], left_a, right_a, across_a, end)
    left_c, right_c, across_c = move(own_c, "x+"), move(own_c, "x-"), move(own_c, "zl")

    segs, plus, minus, waits, owns = [], [], [], [], []

    def late_of(k):
        return waits[k][0], plus[k], waits[k][1], minus[k]

    def send(to_plus, to_minus):
        plus.append(move(to_plus, "y+"))
        minus.append(move(to_minus, "y-"))

    def chunk(pieces, before=(), first=()):
        to_plus, to_minus, *wait, own = fitted_chunk(place, pieces, factors, (*before, *owns[-1:]))
        if owns:
            to_plus, to_minus = messages((to_plus, to_minus), late_of(-1), first)
        send(to_plus, to_minus)
        segs.append(sum(piece.shape[0] for piece in pieces) // 8)
        waits.append(wait)
        owns.append(own)

    kept, arrived = [], []

    def share(k, earlier=()):
        seg = segs[k]
        start = 2 * segs[k + 1] if k + 1 < len(segs) else 0
        terms = [
            [(owns[k], 0, seg), (minus[k], seg, seg), (plus[k + 1], start, seg)],
            [(owns[k], seg, seg), (plus[k], seg, seg), (minus[k + 1], start, seg)],
        ]
        kept.append(shard_sum(terms, earlier))
        arrived.append(move(kept[-1], "zh"))

    chunk((own_a, own_c, left_a, right_a, across_a))
    across_a, right_a = after([across_a, right_a], left_c, right_c, across_c, owns[-1])
    left2_a, far_a, right2_a = move(across_a, "x+"), move(right_a, "x-"), move(right_a, "zl")
    chunk((left_c, right_c, across_c))
    across_c, right_c = after([across_c, right_c], left2_a, far_a, right2_a, owns[-1])
    left2_c, far_c, right2_c = move(across_c, "x+"), move(right_c, "x-"), move(right_c, "zl")
    chunk((left2_a, far_a, right2_a))
    left2_a, right2_c = after([left2_a, right2_c], left2_c, far_c, owns[-1])
    far2 = (move(left2_a, "x+"), move(right2_c, "x-"))
    share(0, (left2_c, far_c, right2_c))
    chunk((left2_c, far_c, right2_c), (kept[0],))
    share(1)
    chunk(far2, (kept[1],), (arrived[0], arrived[1]))
    share(2)
    send(*messages((), late_of(-1), (kept[2],)))
    share(3)
    share(4, (kept[3], arrived[2]))
    base = exchange_partial(place, kept[:2], arrived[:2], factor, ())
    other, *parts = exchange_partial(place, kept[2:], arrived[2:], factor, base)
    other = move(other, "core")
    parts = [part + other[k * BLK : (k + 1) * BLK] for k, part in enumerate(parts)]
    block = parts[-1]
    for part in [move(part, name) for part, name in zip(parts, ("y+", "y-", "y2"))]:
        block = block + part
    for name in ("zl", "xa", "xb"):
        block = block + move(block, name)
    other = move(block, "core")
    low = jnp.where(core == 0, block, other)
    high = jnp.where(core == 0, other, block)
    return jnp.concatenate([low, high], axis=1)


def solution(mesh):
    placed = (P("aux", None, "orb"), P("orb", "aux"), P("aux", None, "orb"), P("orb", "aux"))
    return jax.shard_map(
        body, mesh=mesh, in_specs=placed, out_specs=P("orb", None), check_vma=False
    )
```
